32 devices in a mesh: dp: 4 (over y, core), ctx: 8 (over z, x).
Axes of the slice: x: 2, y: 2, z: 4, core: 2. Of those that a mesh axis runs over, the one named last changes fastest.
Arguments:
- queries: bfloat16 [4, 6144, 2048], P('dp', 'ctx'), may hold values from -6 to 6
- keys: bfloat16 [4, 6144, 2048], P('dp', 'ctx'), may hold values from -6 to 6
- values: bfloat16 [4, 6144, 2048], P('dp', 'ctx'), may hold values from -6 to 6
- grad_out: bfloat16 [4, 6144, 2048], P('dp', 'ctx'), may hold values from -6 to 6
- node_ids: int32 [4, 6144], P('dp', 'ctx'), may hold values from 0 to 383, never falling along the last dimension, each value on 1 to 64 neighbouring positions
- flags: int32 [4, 6144], P('dp', 'ctx'), may hold values 0 or 1
- gain: float32 [16], replicated, may hold values from 0.1 to 1.9
Outputs:
- grad_queries: bfloat16 [4, 6144, 2048], P('dp', 'ctx')
- grad_keys: bfloat16 [4, 6144, 2048], P('dp', 'ctx')
- grad_values: bfloat16 [4, 6144, 2048], P('dp', 'ctx')
- grad_gain: float32 [16], replicated
The draws below stay inside these ranges and needn't reach their ends.
Inputs may be any that keep to these rules, and one draw needn't show every extreme that they name: `node_ids`: node numbers never fall along the tokens of a repository; a node spans 1 to 64 tokens.
All inputs are finite; a program needn't handle non-finite values. No bound on the sum of `flags` on one device may be relied on, other than what follows from the above.
Results may differ from the reference program's by a relative error of at most 0.0049.
Values sent between devices are 32-bit elements; how exact they have to be, the bound alone decides.
A program may use at most 128 MiB of HBM per device.

```python
import math
import jax
import jax.numpy as jnp
import numpy as np
from jax import lax

H = 16
HD = 128
BLOCK = 128
REPOS = 4
TOKENS = 6144
FEAT = 2048
N_DP = 4


def with_ends(drawn, stream_key, smallest, largest):
    spot = [jax.random.randint(jax.random.fold_in(stream_key, axis), (), 0, length) for axis, length in enumerate(drawn.shape)]
    widest = drawn.shape.index(max(drawn.shape))
    next_to = spot[:widest] + [(spot[widest] + 1) % drawn.shape[widest]] + spot[widest + 1:]
    return drawn.at[tuple(spot)].set(smallest).at[tuple(next_to)].set(largest)


def block_scale(key, shape, shards, low, high):
    loudness, own = 1.0, jax.random.fold_in(key, 6)
    for axis_at, parts in shards:
        steps = jnp.exp(jax.random.uniform(jax.random.fold_in(own, axis_at), (parts,), jnp.float32, low / len(shards), high / len(shards)))
        loudness = loudness * jnp.repeat(steps, shape[axis_at] // parts).reshape([-1 if axis == axis_at else 1 for axis in range(len(shape))])
    return loudness


def split_up(count, total, reach, lean):
    portions = [(1 << 20) // math.isqrt(grade ** lean) + 1 for grade in range(2, count + 1)]
    rest, counts = total - reach - (count - 1), [1] * (count - 1)
    while rest > 0:
        free = [i for i in range(count - 1) if counts[i] < reach]
        pool, budget = sum([portions[i] for i in free]), rest
        for i in free:
            addition = min(reach - counts[i], max(1, budget * portions[i] // pool), rest)
            counts[i] = counts[i] + addition
            rest = rest - addition
    return np.array([reach] + counts)


def ragged_sizes(own_key, count, total, reach, lean):
    if count == 2:
        one = jax.random.randint(own_key, (), max(1, total - reach), min(reach, total - 1) + 1)
        return jnp.stack([one, total - one])
    sizes = jnp.asarray(split_up(count, total, reach, lean), jnp.int32)
    couples = (count - 1) // 2
    giver, receiver = sizes[1:1 + 2 * couples:2], sizes[2:2 + 2 * couples:2]
    room = jnp.minimum(giver - 1, reach - receiver)
    passed = jax.random.randint(jax.random.fold_in(own_key, 1), (couples,), 0, 1 << 20) % (room + 1)
    sizes = sizes.at[1:1 + 2 * couples:2].set(giver - passed).at[2:2 + 2 * couples:2].set(receiver + passed)
    return sizes[jax.random.permutation(jax.random.fold_in(own_key, 2), count)]


def noise(stream_key, dims, spread, limit, cuts=(), held_as=jnp.bfloat16):
    entries = jax.random.normal(stream_key, dims, jnp.float32) * spread
    if len(cuts) > 0:
        entries = block_scale(stream_key, dims, cuts, -0.22, 0.18) * entries
    return jnp.clip(entries, min=-limit, max=limit).astype(held_as)


def setup_inputs(seed: int = 0) -> dict:
    seeds = jax.random.split(jax.random.key(seed), 8)
    queries = noise(seeds[0], (REPOS, TOKENS, FEAT), 1.0, 6.0, ((0, 4), (1, 8)))
    keys = noise(seeds[1], (REPOS, TOKENS, FEAT), 1.0, 6.0, ((0, 4), (1, 8)))
    values = noise(seeds[2], (REPOS, TOKENS, FEAT), 1.0, 6.0, ((0, 4), (1, 8)))
    grad_out = noise(seeds[3], (REPOS, TOKENS, FEAT), 1.0, 6.0, ((0, 4), (1, 8)))
    node_ids = jax.vmap(lambda own: jnp.searchsorted(jnp.cumsum(ragged_sizes(own, TOKENS // 16, TOKENS, 64, 1)), jnp.arange(TOKENS), side="right"))(jax.random.split(seeds[4], REPOS)).reshape((REPOS, TOKENS)).astype(jnp.int32)
    flags = with_ends((jax.random.randint(seeds[5], (REPOS, TOKENS), 0, 8) < 1).astype(jnp.int32), jax.random.fold_in(seeds[5], 1), 0, 1)
    gain = jnp.clip(1.0 + 0.18 * jax.random.normal(seeds[6], (H,), jnp.float32), 0.1, 1.9)
    return {"queries": queries, "keys": keys, "values": values, "grad_out": grad_out, "node_ids": node_ids, "flags": flags, "gain": gain}


def to_half(array):
    rounded = array.astype(jnp.bfloat16)
    rounded = lax.optimization_barrier(rounded)
    return rounded.astype(jnp.float32)

def one_repo(items):
    queries, keys, values, grad_out, node_ids, flags, gain = items
    count = TOKENS // BLOCK
    scale = 1.0 / math.sqrt(HD * TOKENS)
    q_blk = queries.reshape(count, BLOCK, H, HD).astype(jnp.float32)
    k_blk = keys.reshape(count, BLOCK, H, HD).astype(jnp.float32)
    v_blk = values.reshape(count, BLOCK, H, HD).astype(jnp.float32)
    g_blk = grad_out.reshape(count, BLOCK, H, HD).astype(jnp.float32)
    nodes = node_ids.reshape(count, BLOCK)
    marks = flags.reshape(count, BLOCK)
    rows = lax.broadcasted_iota(jnp.int32, (BLOCK, BLOCK), 0)
    cols = lax.broadcasted_iota(jnp.int32, (BLOCK, BLOCK), 1)
    causal = (cols <= rows)[None]
    linked = (nodes[:, :, None] == nodes[:, None, :]) | (marks[:, None, :] == 1)
    seen = (causal & linked).astype(jnp.float32)[:, None]
    scores = jnp.einsum('bthd,bshd->bhts', q_blk, k_blk) * seen
    dscores = jnp.einsum('bthd,bshd->bhts', g_blk, v_blk) * seen
    intra_term = lax.optimization_barrier(jnp.sum(scores * dscores, axis=(0, 2, 3)))
    pm = to_half(scores)
    dpm = to_half(dscores)
    kv_blk = jnp.einsum('bshd,bshe->bhde', k_blk, v_blk)
    qg_blk = jnp.einsum('bthd,bthe->bhde', q_blk, g_blk)
    zero = jnp.zeros((1,) + kv_blk.shape[1:], jnp.float32)
    prior = jnp.cumsum(jnp.concatenate([zero, kv_blk[:-1]], axis=0), axis=0)
    later = jnp.flip(jnp.cumsum(jnp.flip(jnp.concatenate([qg_blk[1:], zero], axis=0), 0), axis=0), 0)
    inter_term = lax.optimization_barrier(jnp.sum(prior * qg_blk, axis=(0, 2, 3)))
    prior_h = to_half(prior)
    later_h = to_half(later)
    factor = (scale * gain)[None, None, :, None]
    dq = jnp.einsum('bhts,bshd->bthd', dpm, k_blk) + jnp.einsum('bthe,bhde->bthd', g_blk, prior_h)
    dk = jnp.einsum('bhts,bthd->bshd', dpm, q_blk) + jnp.einsum('bshe,bhde->bshd', v_blk, later_h)
    dv = jnp.einsum('bhts,bthd->bshd', pm, g_blk) + jnp.einsum('bshd,bhde->bshe', k_blk, later_h)
    shape = (TOKENS, H * HD)
    return ((dq * factor).astype(jnp.bfloat16).reshape(shape), (dk * factor).astype(jnp.bfloat16).reshape(shape), (dv * factor).astype(jnp.bfloat16).reshape(shape), scale * (intra_term + inter_term))

def reference(queries, keys, values, grad_out, node_ids, flags, gain):
    repos = queries.shape[0]
    gains = jnp.broadcast_to(gain, (repos,) + gain.shape)
    dq, dk, dv, terms = lax.map(one_repo, (queries, keys, values, grad_out, node_ids, flags, gains))
    grad_gain = lax.optimization_barrier(jnp.sum(terms, axis=0)) / math.sqrt(N_DP * TOKENS * HD)
    return (dq, dk, dv, grad_gain.astype(jnp.float32))
```

```python
import math

import jax
import jax.numpy as jnp
from jax import lax
from jax.experimental import pallas as pl
from jax.experimental.pallas import tpu as pltpu
from jax.sharding import PartitionSpec as P

H = 16
HD = 128
BLOCK = 128
PER = 2
CHUNKS = 2


def nt(a, b):
    return lax.dot_general(a, b, (((1,), (1,)), ((), ())), preferred_element_type=jnp.float32)


def tn(a, b):
    return lax.dot_general(a, b, (((0,), (0,)), ((), ())), preferred_element_type=jnp.float32)


def nn(a, b):
    return lax.dot_general(a, b, (((1,), (0,)), ((), ())), preferred_element_type=jnp.float32)


def cols(i):
    return slice(i * HD, (i + 1) * HD)


def state_kernel(q_ref, k_ref, v_ref, g_ref, kv_ref, qg_ref):
    for i in range(PER):
        kv_ref[i] = tn(k_ref[0, :, cols(i)], v_ref[0, :, cols(i)])
        qg_ref[i] = tn(q_ref[0, :, cols(i)], g_ref[0, :, cols(i)])


def term_kernel(q_ref, k_ref, v_ref, g_ref, seen_ref, term_ref):
    count = q_ref.shape[1] // BLOCK
    for i in range(PER):
        total = jnp.zeros((BLOCK, HD), jnp.float32)
        state = jnp.zeros((HD, HD), jnp.float32)
        for b in range(count):
            at = (0, slice(b * BLOCK, (b + 1) * BLOCK), cols(i))
            q, k, v, g = q_ref[at], k_ref[at], v_ref[at], g_ref[at]
            total = total + nt(q, k) * nt(g, v) * seen_ref[b]
            if b > 0:
                total = total + state * tn(q, g)
            if b < count - 1:
                state = state + tn(k, v)
        term_ref[i] = jnp.sum(total, axis=0, keepdims=True)


def grad_kernel(q_ref, k_ref, v_ref, g_ref, seen_ref, prior_ref, later_ref, factor_ref,
                dq_ref, dk_ref, dv_ref):
    count = q_ref.shape[1] // BLOCK
    step = pl.program_id(0)
    for i in range(PER):
        factor = factor_ref[step * PER + i]
        later = [later_ref[i]]
        for b in range(count - 1, 0, -1):
            at = (0, slice(b * BLOCK, (b + 1) * BLOCK), cols(i))
            later.append(later[-1] + tn(q_ref[at], g_ref[at]))
        later = [r.astype(jnp.bfloat16) for r in later[::-1]]
        prior = prior_ref[i]
        for b in range(count):
            at = (0, slice(b * BLOCK, (b + 1) * BLOCK), cols(i))
            q, k, v, g = q_ref[at], k_ref[at], v_ref[at], g_ref[at]
            seen = seen_ref[b]
            pm = (nt(q, k) * seen).astype(jnp.bfloat16)
            dpm = (nt(g, v) * seen).astype(jnp.bfloat16)
            s = prior.astype(jnp.bfloat16)
            r = later[b]
            dq_ref[at] = ((nn(dpm, k) + nt(g, s)) * factor).astype(jnp.bfloat16)
            dk_ref[at] = ((tn(dpm, q) + nt(v, r)) * factor).astype(jnp.bfloat16)
            dv_ref[at] = ((tn(pm, g) + nn(k, r)) * factor).astype(jnp.bfloat16)
            if b < count - 1:
                prior = prior + tn(k, v)


def cost(heads, length, products, extra):
    return pl.CostEstimate(
        flops=2 * heads * length * HD * HD * products,
        bytes_accessed=8 * heads * length * HD + extra,
        transcendentals=0,
    )


PARAMS = pltpu.CompilerParams(vmem_limit_bytes=40 * 1024 * 1024)


def on_device(queries, keys, values, grad_out, node_ids, flags, gain):
    length = queries.shape[1]
    count = length // BLOCK
    n = lax.axis_size("ctx")
    place = lax.axis_index("ctx")
    scale = 1.0 / math.sqrt(HD * length * n)
    tokens = (queries, keys, values, grad_out)

    def wide(first):
        return pl.BlockSpec((1, length, PER * HD), lambda i: (0, 0, i + first))

    state_spec = pl.BlockSpec((PER, HD, HD), lambda i: (i, 0, 0))
    group = H // CHUNKS
    states = []
    for c in range(CHUNKS):
        states.append(pl.pallas_call(
            state_kernel,
            grid=(group // PER,),
            in_specs=[wide(c * group // PER)] * 4,
            out_specs=[state_spec] * 2,
            out_shape=[jax.ShapeDtypeStruct((group, HD, HD), jnp.float32)] * 2,
            compiler_params=PARAMS,
            cost_estimate=cost(group, length, 2, 8 * group * HD * HD),
            name="states",
        )(*tokens))

    side = 2 if n % 2 == 0 else 1
    odd = (place % side) == 1
    swap = [(i, i ^ 1) for i in range(n)]
    up = [(i, i + side) for i in range(n - side)]
    down = [(i + side, i) for i in range(n - side)]
    priors, laters = [], []
    for kv, qg in states:
        if side == 2:
            kv_other = lax.ppermute(kv, "ctx", swap)
            qg_other = lax.ppermute(qg, "ctx", swap)
            prior = jnp.where(odd, kv_other, 0.0)
            later = jnp.where(odd, 0.0, qg_other)
            kv_move, qg_move = kv + kv_other, qg + qg_other
        else:
            prior, later = jnp.zeros_like(kv), jnp.zeros_like(qg)
            kv_move, qg_move = kv, qg
        for _ in range(n // side - 1):
            kv_move = lax.ppermute(kv_move, "ctx", up)
            qg_move = lax.ppermute(qg_move, "ctx", down)
            prior = prior + kv_move
            later = later + qg_move
        priors.append(prior)
        laters.append(later)

    nodes = node_ids.reshape(count, BLOCK)
    marks = flags.reshape(count, BLOCK)
    row = lax.broadcasted_iota(jnp.int32, (BLOCK, BLOCK), 0)
    col = lax.broadcasted_iota(jnp.int32, (BLOCK, BLOCK), 1)
    linked = (nodes[:, :, None] == nodes[:, None, :]) | (marks[:, None, :] == 1)
    seen = ((col <= row)[None] & linked).astype(jnp.float32)
    seen_spec = pl.BlockSpec((count, BLOCK, BLOCK), lambda i: (0, 0, 0))

    near = pl.pallas_call(
        term_kernel,
        grid=(H // PER,),
        in_specs=[wide(0)] * 4 + [seen_spec],
        out_specs=pl.BlockSpec((PER, 1, HD), lambda i: (i, 0, 0)),
        out_shape=jax.ShapeDtypeStruct((H, 1, HD), jnp.float32),
        compiler_params=PARAMS,
        cost_estimate=cost(H, length, 8, 0),
        name="gain_term",
    )(*tokens, seen)

    far = jnp.concatenate([
        jnp.sum(prior * qg, axis=(1, 2)) for prior, (_, qg) in zip(priors, states)
    ])
    term = scale * (jnp.sum(near, axis=(1, 2)) + far)
    total = lax.psum(term, ("dp", "ctx"))

    wide_out = jax.ShapeDtypeStruct(queries.shape, jnp.bfloat16)
    grads = pl.pallas_call(
        grad_kernel,
        grid=(H // PER,),
        in_specs=[wide(0)] * 4 + [seen_spec, state_spec, state_spec,
                                  pl.BlockSpec(memory_space=pltpu.SMEM)],
        out_specs=[wide(0)] * 3,
        out_shape=[wide_out] * 3,
        compiler_params=PARAMS,
        cost_estimate=cost(H, length, 20, 6 * H * length * HD),
        name="grads",
    )(*tokens, seen, jnp.concatenate(priors), jnp.concatenate(laters), scale * gain)

    norm_tokens = lax.axis_size("dp") * length * n * HD
    grad_gain = (total / math.sqrt(norm_tokens)).astype(jnp.float32)
    return (*grads, grad_gain)


def solution(mesh):
    rows = P("dp", "ctx", None)
    return jax.shard_map(
        on_device,
        mesh=mesh,
        in_specs=(rows, rows, rows, rows, P("dp", "ctx"), P("dp", "ctx"), P()),
        out_specs=(rows, rows, rows, P()),
        check_vma=False,
    )
```

```python
import math

import jax
import jax.numpy as jnp
from jax import lax
from jax.experimental import pallas as pl
from jax.experimental.pallas import tpu as pltpu
from jax.sharding import PartitionSpec as P

H = 16
HD = 128
BLOCK = 128
PER = 2
CHUNKS = 2


def nt(a, b):
    return lax.dot_general(a, b, (((1,), (1,)), ((), ())), preferred_element_type=jnp.float32)


def tn(a, b):
    return lax.dot_general(a, b, (((0,), (0,)), ((), ())), preferred_element_type=jnp.float32)


def nn(a, b):
    return lax.dot_general(a, b, (((1,), (0,)), ((), ())), preferred_element_type=jnp.float32)


def cols(i):
    return slice(i * HD, (i + 1) * HD)


def state_kernel(q_ref, k_ref, v_ref, g_ref, kv_ref, qg_ref):
    for i in range(PER):
        kv_ref[i] = tn(k_ref[0, :, cols(i)], v_ref[0, :, cols(i)])
        qg_ref[i] = tn(q_ref[0, :, cols(i)], g_ref[0, :, cols(i)])


def term_kernel(q_ref, k_ref, v_ref, g_ref, seen_ref, term_ref):
    count = q_ref.shape[1] // BLOCK
    for i in range(PER):
        total = jnp.zeros((BLOCK, HD), jnp.float32)
        state = jnp.zeros((HD, HD), jnp.float32)
        for b in range(count):
            at = (0, slice(b * BLOCK, (b + 1) * BLOCK), cols(i))
            q, k, v, g = q_ref[at], k_ref[at], v_ref[at], g_ref[at]
            total = total + nt(q, k) * nt(g, v) * seen_ref[b]
            if b > 0:
                total = total + state * tn(q, g)
            if b < count - 1:
                state = state + tn(k, v)
        term_ref[i] = jnp.sum(total, axis=0, keepdims=True)


def grad_kernel(q_ref, k_ref, v_ref, g_ref, seen_ref, prior_ref, later_ref, factor_ref,
                dq_ref, dk_ref, dv_ref):
    count = q_ref.shape[1] // BLOCK
    step = pl.program_id(0)
    for i in range(PER):
        factor = factor_ref[step * PER + i]
        later = [later_ref[i]]
        for b in range(count - 1, 0, -1):
            at = (0, slice(b * BLOCK, (b + 1) * BLOCK), cols(i))
            later.append(later[-1] + tn(q_ref[at], g_ref[at]))
        later = [r.astype(jnp.bfloat16) for r in later[::-1]]
        prior = prior_ref[i]
        for b in range(count):
            at = (0, slice(b * BLOCK, (b + 1) * BLOCK), cols(i))
            q, k, v, g = q_ref[at], k_ref[at], v_ref[at], g_ref[at]
            seen = seen_ref[b]
            pm = (nt(q, k) * seen).astype(jnp.bfloat16)
            dpm = (nt(g, v) * seen).astype(jnp.bfloat16)
            s = prior.astype(jnp.bfloat16)
            r = later[b]
            dq_ref[at] = ((nn(dpm, k) + nt(g, s)) * factor).astype(jnp.bfloat16)
            dk_ref[at] = ((tn(dpm, q) + nt(v, r)) * factor).astype(jnp.bfloat16)
            dv_ref[at] = ((tn(pm, g) + nn(k, r)) * factor).astype(jnp.bfloat16)
            if b < count - 1:
                prior = prior + tn(k, v)


def cost(heads, length, products, extra):
    return pl.CostEstimate(
        flops=2 * heads * length * HD * HD * products,
        bytes_accessed=8 * heads * length * HD + extra,
        transcendentals=0,
    )


PARAMS = pltpu.CompilerParams(vmem_limit_bytes=60 * 1024 * 1024)


def on_device(queries, keys, values, grad_out, node_ids, flags, gain):
    length = queries.shape[1]
    count = length // BLOCK
    n = lax.axis_size("ctx")
    place = lax.axis_index("ctx")
    scale = 1.0 / math.sqrt(HD * length * n)
    tokens = (queries, keys, values, grad_out)

    def wide(first):
        return pl.BlockSpec((1, length, PER * HD), lambda i: (0, 0, i + first))

    state_spec = pl.BlockSpec((PER, HD, HD), lambda i: (i, 0, 0))
    group = H // CHUNKS
    states = []
    for c in range(CHUNKS):
        states.append(pl.pallas_call(
            state_kernel,
            grid=(group // PER,),
            in_specs=[wide(c * group // PER)] * 4,
            out_specs=[state_spec] * 2,
            out_shape=[jax.ShapeDtypeStruct((group, HD, HD), jnp.float32)] * 2,
            compiler_params=PARAMS,
            cost_estimate=cost(group, length, 2, 8 * group * HD * HD),
            name="states",
        )(*tokens))

    side = 2 if n % 2 == 0 else 1
    odd = (place % side) == 1
    swap = [(i, i ^ 1) for i in range(n)]
    up = [(i, i + side) for i in range(n - side)]
    down = [(i + side, i) for i in range(n - side)]
    priors, laters = [], []
    for kv, qg in states:
        if side == 2:
            kv_other = lax.ppermute(kv, "ctx", swap)
            qg_other = lax.ppermute(qg, "ctx", swap)
            prior = jnp.where(odd, kv_other, 0.0)
            later = jnp.where(odd, 0.0, qg_other)
            kv_move, qg_move = kv + kv_other, qg + qg_other
        else:
            prior, later = jnp.zeros_like(kv), jnp.zeros_like(qg)
            kv_move, qg_move = kv, qg
        for _ in range(n // side - 1):
            kv_move = lax.ppermute(kv_move, "ctx", up)
            qg_move = lax.ppermute(qg_move, "ctx", down)
            prior = prior + kv_move
            later = later + qg_move
        priors.append(prior)
        laters.append(later)

    nodes = node_ids.reshape(count, BLOCK)
    marks = flags.reshape(count, BLOCK)
    row = lax.broadcasted_iota(jnp.int32, (BLOCK, BLOCK), 0)
    col = lax.broadcasted_iota(jnp.int32, (BLOCK, BLOCK), 1)
    linked = (nodes[:, :, None] == nodes[:, None, :]) | (marks[:, None, :] == 1)
    seen = ((col <= row)[None] & linked).astype(jnp.float32)
    seen_spec = pl.BlockSpec((count, BLOCK, BLOCK), lambda i: (0, 0, 0))

    near = pl.pallas_call(
        term_kernel,
        grid=(H // PER,),
        in_specs=[wide(0)] * 4 + [seen_spec],
        out_specs=pl.BlockSpec((PER, 1, HD), lambda i: (i, 0, 0)),
        out_shape=jax.ShapeDtypeStruct((H, 1, HD), jnp.float32),
        compiler_params=PARAMS,
        cost_estimate=cost(H, length, 8, 0),
        name="gain_term",
    )(*tokens, seen)

    far = jnp.concatenate([
        jnp.sum(prior * qg, axis=(1, 2)) for prior, (_, qg) in zip(priors, states)
    ])
    term = scale * (jnp.sum(near, axis=(1, 2)) + far)
    total = jnp.sum(lax.all_gather(term, ("dp", "ctx")), axis=0)

    wide_out = jax.ShapeDtypeStruct(queries.shape, jnp.bfloat16)
    grads = pl.pallas_call(
        grad_kernel,
        grid=(H // PER,),
        in_specs=[wide(0)] * 4 + [seen_spec, state_spec, state_spec,
                                  pl.BlockSpec(memory_space=pltpu.SMEM)],
        out_specs=[wide(0)] * 3,
        out_shape=[wide_out] * 3,
        compiler_params=PARAMS,
        cost_estimate=cost(H, length, 20, 6 * H * length * HD),
        name="grads",
    )(*tokens, seen, jnp.concatenate(priors), jnp.concatenate(laters), scale * gain)

    norm_tokens = lax.axis_size("dp") * length * n * HD
    grad_gain = (total / math.sqrt(norm_tokens)).astype(jnp.float32)
    return (*grads, grad_gain)


def solution(mesh):
    rows = P("dp", "ctx", None)
    return jax.shard_map(
        on_device,
        mesh=mesh,
        in_specs=(rows, rows, rows, rows, P("dp", "ctx"), P("dp", "ctx"), P()),
        out_specs=(rows, rows, rows, P()),
        check_vma=False,
    )
```
